512 devices in a mesh: ctx: 16 (over z_lo, core), tp: 32 (over z_hi, x, y).
Axes of the slice: x: 4, y: 4, z: 16 (z_hi: 2, z_lo: 8; z = z_hi * 8 + z_lo), core: 2. Of those that a mesh axis runs over, the one named last changes fastest.
Arguments:
- residual: bfloat16 [4096, 8192], P('ctx', 'tp'), may hold values from -8 to 8
- queries: bfloat16 [4096, 8192], P('ctx', 'tp'), may hold values from -15 to 15
- keys_values: bfloat16 [4096, 2048], P('ctx'), may hold values from -6 to 6
- out_weight: bfloat16 [8192, 8192], P('tp', 'ctx'), may hold values from -0.125 to 0.125
- norm_gain: float32 [8192], replicated, may hold values from 0.1 to 1.9
- cache_weight: bfloat16 [8192, 2048], P(None, 'tp'), may hold values from -0.0625 to 0.0625
- positions: int32 [4096], P('ctx'), may hold values from 0 to 8191, as said below
- keep_rows: int32 [4096], P('ctx'), may hold values from 0 to 255, as said below
- kept_count: int32 [16], P('ctx'), may hold values from 64 to 256, as said below
Outputs:
- kept_hidden: bfloat16 [4096, 8192], P('ctx', 'tp')
- kept_cache: bfloat16 [4096, 2048], P('ctx', 'tp')
The draws below stay inside these ranges and needn't reach their ends.
Inputs may be any that keep to these rules, and one draw needn't show every extreme that they name: `keep_rows`: within every shard of ctx the 256 entries are a permutation of the shard's local rows: first its kept rows in ascending order, as many as its kept_count, then its dropped rows in ascending order. `kept_count`: for every even shard index e, shards e and e + 1 keep 2 * 160 rows together. `positions`: strictly increasing along the tokens.
All inputs are finite; a program needn't handle non-finite values.
Results may differ from the reference program's by a relative error of at most 0.019.
Values may be sent and summed in bfloat16 or wider, within the bound.
No kernel may reach another device: no remote copies, remote signals or barrier semaphores. Data moves between devices by JAX's collectives and lax.ppermute only.
A program may use at most 64 MiB of HBM per device.

```python
import math
import jax
import jax.numpy as jnp
from jax import lax

D = 8192
HQ = 64
KVH = 8
HD = 128
TOK_DEV = 256
DROP_DEV = 96
TOKENS = 4096
N_CTX = 16
N_TP = 32


def drop_counts(key):
    shards = TOKENS // TOK_DEV
    pair_total = shards // 2
    spread = jax.random.randint(jax.random.fold_in(key, 7), (pair_total,), 0, DROP_DEV + 1)
    widest = jax.random.randint(jax.random.fold_in(key, 8), (), 0, pair_total)
    spread = jnp.where(jnp.arange(pair_total) == widest, DROP_DEV, spread)
    heavy_first = jax.random.randint(jax.random.fold_in(key, 9), (pair_total,), 0, 2)
    first_drop = jnp.where(heavy_first == 1, DROP_DEV - spread, DROP_DEV + spread)
    second_drop = 2 * DROP_DEV - first_drop
    return jnp.stack([first_drop, second_drop], -1).reshape(shards).astype(jnp.int32)


def draw_kept_count(key, part):
    drop_list = drop_counts(key)
    return (TOK_DEV - drop_list).astype(jnp.int32)


def draw_keep_rows(key, part):
    drop_list = drop_counts(key)
    key = jax.random.fold_in(key, 5)
    shards = TOKENS // TOK_DEV
    rank_rows = jax.vmap(lambda sub_key: jax.random.permutation(sub_key, TOK_DEV))(jax.random.split(key, shards))
    dropped = (rank_rows < drop_list[:, None]).astype(jnp.int32)
    sort_key = dropped * TOK_DEV + jnp.arange(TOK_DEV, dtype=jnp.int32)[None, :]
    return jnp.argsort(sort_key, axis=1, stable=True).astype(jnp.int32).reshape(TOKENS)


def draw_positions(key, part):
    key = jax.random.fold_in(key, 3)
    step_size = jax.random.randint(key, (TOKENS,), 0, 2)
    step_size = step_size.at[0].set(0).at[TOKENS - 1].set(1)
    return (2 * jnp.arange(TOKENS, dtype=jnp.int32) + step_size).astype(jnp.int32)


def draw_residual(key, part):
    key = jax.random.fold_in(key, 11)
    column = 0.5 * jnp.power(3.0, jnp.arange(D, dtype=jnp.float32) / (D - 1))
    base_draw = jnp.clip(jax.random.normal(key, (TOKENS, D), jnp.float32), -4.0, 4.0)
    return (base_draw * column[None, :]).astype(jnp.bfloat16)


def draw_queries(key, part):
    key = jax.random.fold_in(key, 21)
    base_draw = jnp.clip(2.5 * jax.random.normal(key, (TOKENS, HQ, HD), jnp.float32), -15.0, 15.0)
    return base_draw.reshape(TOKENS, HQ * HD).astype(jnp.bfloat16)


def draw_keys_values(key, part):
    key = jax.random.fold_in(key, 31)
    base_draw = jnp.clip(jax.random.normal(key, (TOKENS, KVH, 2, HD), jnp.float32), -6.0, 6.0)
    return base_draw.reshape(TOKENS, KVH * 2 * HD).astype(jnp.bfloat16)


def with_spikes(result, own_key, source, target, shards_of, factor):
    owner, partner = [(jnp.arange(result.shape[dim]) // (result.shape[dim] // shards_of)).reshape([-1 if axis == dim else 1 for axis in range(result.ndim)]) for dim in (source, target)]
    chosen = jax.random.permutation(own_key, shards_of)[partner]
    strong = (owner == chosen) | (owner == (partner + shards_of // 2) % shards_of)
    return jnp.where(strong, factor * result, result)


def levels(key, extent, cuts, smallest, high):
    def one(axis_at, blocks):
        heights = jax.random.uniform(jax.random.fold_in(jax.random.fold_in(key, 6), axis_at), (blocks,), jnp.float32, smallest / len(cuts), high / len(cuts))
        return jnp.repeat(jnp.exp(heights), extent[axis_at] // blocks).reshape((-1,) + (1,) * (len(extent) - axis_at - 1))

    level = one(*cuts[0])
    for cut in cuts[1:]:
        level = level * one(*cut)
    return level


def gaussian(rng, shape, deviation, limit, pieces=(), held_as=jnp.bfloat16):
    drawn = jax.random.normal(rng, shape, jnp.float32) * deviation
    if len(pieces) > 0:
        drawn = levels(rng, shape, pieces, -0.22, 0.18) * drawn
    return jnp.clip(drawn, min=-limit, max=limit).astype(held_as)


def gaussian_with(key, dims, width, bound, cuts, heavy, held_as=jnp.bfloat16):
    array = width * jax.random.normal(key, dims, jnp.float32)
    if cuts:
        array = array * levels(key, dims, cuts, -0.22, 0.18)
    return jnp.clip(with_spikes(array, jax.random.fold_in(key, 3), *heavy), -bound, bound).astype(held_as)


def setup_inputs(seed: int = 0) -> dict:
    splits = jax.random.split(jax.random.key(seed), 10)
    residual = draw_residual(jax.random.fold_in(splits[9], 71), 0)
    queries = draw_queries(jax.random.fold_in(splits[9], 71), 0)
    keys_values = draw_keys_values(jax.random.fold_in(splits[9], 71), 0)
    out_weight = gaussian_with(splits[3], (HQ * HD, D), (HQ * HD) ** -0.5, 0.125, ((0, 32), (1, 16)), (0, 1, 32, 2.75))
    norm_gain = jnp.clip(1.0 + 0.18 * jax.random.normal(splits[4], (D,), jnp.float32), 0.1, 1.9)
    cache_weight = gaussian(splits[5], (D, KVH * 2 * HD), D ** -0.5, 0.0625, ((1, 32),))
    positions = draw_positions(jax.random.fold_in(splits[9], 71), 0)
    keep_rows = draw_keep_rows(jax.random.fold_in(splits[9], 71), 0)
    kept_count = draw_kept_count(jax.random.fold_in(splits[9], 71), 0)
    return dict(residual=residual, queries=queries, keys_values=keys_values, out_weight=out_weight, norm_gain=norm_gain, cache_weight=cache_weight, positions=positions, keep_rows=keep_rows, kept_count=kept_count)


THETA = 1000000.0
EPS = 1e-06

def rotate_pairs(cache_rows, position_ids, first_col, head_dim):
    pair_count = cache_rows.shape[1] // 2
    columns = first_col + 2 * jnp.arange(pair_count, dtype=jnp.int32)
    within = columns % (2 * head_dim)
    is_key = within < head_dim
    exponent = jnp.where(is_key, within, 0).astype(jnp.float32) / head_dim
    frequency = jnp.power(jnp.float32(THETA), -exponent)
    angles = position_ids.astype(jnp.float32)[:, None] * frequency[None, :]
    paired = cache_rows.reshape(cache_rows.shape[0], pair_count, 2)
    first_half = paired[..., 0]
    second = paired[..., 1]
    cosine = jnp.cos(angles)
    sine_rows = jnp.sin(angles)
    turned_first = first_half * cosine - second * sine_rows
    turned_second = second * cosine + first_half * sine_rows
    turned = jnp.stack([jnp.where(is_key, turned_first, first_half), jnp.where(is_key, turned_second, second)], -1)
    return turned.reshape(cache_rows.shape)

def reference(residual, queries, keys_values, out_weight, norm_gain, cache_weight, positions, keep_rows, kept_count):
    group_size = HQ // KVH
    score_scale = 1.0 / math.sqrt(HD)
    query_heads = queries.reshape(TOKENS, HQ, HD).transpose(1, 0, 2)
    kv_pairs = keys_values.reshape(TOKENS, KVH, 2, HD)
    key_heads = kv_pairs[:, :, 0, :].transpose(1, 0, 2)
    value_heads = kv_pairs[:, :, 1, :].transpose(1, 0, 2)
    causal = jnp.arange(TOKENS, dtype=jnp.int32)[:, None] >= jnp.arange(TOKENS, dtype=jnp.int32)[None, :]

    def one_head(item_pair):
        query_rows, head_index = item_pair
        key_block = key_heads[head_index // group_size]
        value_block = value_heads[head_index // group_size]
        scores = jnp.dot(query_rows, key_block.T, preferred_element_type=jnp.float32) * score_scale
        scores = jnp.where(causal, scores, -jnp.inf)
        row_max = lax.optimization_barrier(jnp.max(scores, axis=-1, keepdims=True))
        probs = jnp.exp(scores - row_max)
        denominator = lax.optimization_barrier(jnp.sum(probs, axis=-1, keepdims=True))
        mixed_rows = jnp.dot(probs.astype(jnp.bfloat16), value_block, preferred_element_type=jnp.float32) / denominator
        return mixed_rows.astype(jnp.bfloat16)
    attended = lax.map(one_head, (query_heads, jnp.arange(HQ, dtype=jnp.int32)))
    attended = attended.transpose(1, 0, 2).reshape(TOKENS, HQ * HD)
    part_width = HQ * HD // N_TP
    attn_parts = attended.reshape(TOKENS, N_TP, part_width).transpose(1, 0, 2)
    weight_parts = out_weight.reshape(N_TP, part_width, D)

    def add_part(running, item_pair):
        attn_part, weight_part = item_pair
        term_part = jnp.dot(attn_part, weight_part, preferred_element_type=jnp.float32).astype(jnp.bfloat16)
        term_part = lax.optimization_barrier(term_part)
        return (running + term_part.astype(jnp.float32), None)
    summed, unused = lax.scan(add_part, jnp.zeros((TOKENS, D), jnp.float32), (attn_parts, weight_parts))
    hidden = (residual.astype(jnp.float32) + summed).astype(jnp.bfloat16)
    wide_hidden = hidden.astype(jnp.float32)
    inverse = lax.rsqrt(lax.optimization_barrier(jnp.mean(wide_hidden * wide_hidden, axis=-1, keepdims=True)) + EPS)
    normed = (wide_hidden * inverse * norm_gain[None, :]).astype(jnp.bfloat16)
    cache_rows = jnp.dot(normed, cache_weight, preferred_element_type=jnp.float32)
    cache_rot = rotate_pairs(cache_rows, positions, 0, HD).astype(jnp.bfloat16)
    keep_grid = keep_rows.reshape(N_CTX, TOK_DEV)
    valid_rows = (jnp.arange(TOK_DEV, dtype=jnp.int32)[None, :] < kept_count[:, None]).astype(jnp.int32)
    kept_flags = jnp.zeros((N_CTX, TOK_DEV), jnp.int32).at[jnp.arange(N_CTX, dtype=jnp.int32)[:, None], keep_grid].set(valid_rows)
    kept_rows = kept_flags.reshape(TOKENS)[:, None] > 0
    kept_hidden = jnp.where(kept_rows, hidden, jnp.zeros_like(hidden))
    kept_cache = jnp.where(kept_rows, cache_rot, jnp.zeros_like(cache_rot))
    return (kept_hidden, kept_cache)
```

```python
import math

import jax
import jax.numpy as jnp
from jax import lax
from jax.sharding import PartitionSpec as P

D = 8192
HQ = 64
KVH = 8
HD = 128
THETA = 1000000.0
EPS = 1e-06

ZL, CORES, ZH, NX, NY = 8, 2, 2, 4, 4
PAIR_KEEP = 320
OWN = PAIR_KEEP // 2
AXES = ("ctx", "tp")
BF = jnp.bfloat16
F32 = jnp.float32


def pairs(move):
    found = []
    for zl in range(ZL):
        for core in range(CORES):
            for zh in range(ZH):
                target = move(zh, zl, core)
                if target is None:
                    continue
                for plane in range(NX * NY):
                    source = (zl * CORES + core) * (ZH * NX * NY) + zh * NX * NY + plane
                    to = (target[1] * CORES + target[2]) * (ZH * NX * NY) + target[0] * NX * NY + plane
                    found.append((source, to))
    return found


CORE = pairs(lambda zh, zl, core: (zh, zl, 1 - core))
FOUR = pairs(lambda zh, zl, core: (zh, zl ^ 4, core))
EIGHT = pairs(lambda zh, zl, core: (1 - zh, zl, core))
TWELVE = pairs(lambda zh, zl, core: (1 - zh, zl ^ 4, core))
QUAD = [None] + [pairs(lambda zh, zl, core, k=k: (zh, zl ^ k, core)) for k in (1, 2, 3)]
BACK = [None] + [
    pairs(lambda zh, zl, core, k=k: (zh if k <= 4 else 1 - zh, zl + k, core) if zl + k < ZL else None)
    for k in range(1, ZL)
]
PLANES = [[half * NX * NY + i for i in range(NX * NY)] for half in range(ZH)]


def send(x, table):
    return lax.ppermute(x, AXES, table)


def plane_exchange(x):
    return lax.all_to_all(x, "tp", 0, 0, tiled=True, axis_index_groups=PLANES)


def turn(cache_rows, position_ids, first_col):
    column = first_col + jnp.arange(cache_rows.shape[1], dtype=jnp.int32)
    within = column % (2 * HD)
    is_key = within < HD
    exponent = jnp.where(is_key, within - within % 2, 0).astype(F32) / HD
    frequency = jnp.power(F32(THETA), -exponent)
    angles = position_ids[:, None] * frequency[None, :]
    even = (column % 2 == 0)[None, :]
    other = jnp.where(even, -jnp.roll(cache_rows, -1, axis=1), jnp.roll(cache_rows, 1, axis=1))
    turned = cache_rows * jnp.cos(angles) + other * jnp.sin(angles)
    return jnp.where(is_key[None, :], turned, cache_rows)


def shards(
    residual, queries, keys_values, out_weight, norm_gain, cache_weight, positions, keep_rows, kept_count
):
    rows = residual.shape[0]
    ctx = lax.axis_index("ctx")
    tp = lax.axis_index("tp")
    zl, core = ctx // CORES, ctx % CORES
    zh, plane = tp // (NX * NY), tp % (NX * NY)
    first = core == 0

    local = jnp.arange(rows, dtype=jnp.int32)
    order = jnp.where(local < kept_count[0], local, -1)
    hits = keep_rows[:, None] == local[None, :]
    rank = jnp.sum(jnp.where(hits, order[:, None], 0), axis=0)
    meta = jnp.stack([rank, positions // 128, positions % 128], axis=1).astype(BF)
    meta = jnp.pad(meta, ((0, 0), (0, 125)))
    mine = jnp.concatenate([queries, residual, meta], axis=1)
    theirs = send(mine, CORE)

    head = zh * (KVH // ZH) + plane // NY
    far_head = (1 - zh) * (KVH // ZH) + plane // NY
    own_kv = lax.dynamic_slice_in_dim(keys_values, head * 2 * HD, 2 * HD, 1)
    far_kv = lax.dynamic_slice_in_dim(keys_values, far_head * 2 * HD, 2 * HD, 1)
    blocks = [own_kv] + [send(own_kv if k <= 4 else far_kv, BACK[k]) for k in range(1, ZL)]

    weight = jnp.stack([out_weight[:, :256], out_weight[:, 256:]])
    quad = jnp.stack([weight] + [send(weight, QUAD[k]) for k in (1, 2, 3)])
    quad_other = send(quad, CORE)

    columns = cache_weight.shape[1]
    gained = (cache_weight.astype(F32) * norm_gain[:, None]).astype(BF)
    gained = gained.T.reshape(columns, ZH, NX * NY, D // (ZH * NX * NY)).transpose(2, 0, 1, 3)
    gained = plane_exchange(gained.reshape(NX * NY, columns, -1))

    pair = jnp.where(first, jnp.concatenate([mine, theirs]), jnp.concatenate([theirs, mine]))
    pair_rank = pair[:, 512].astype(jnp.int32)
    count0 = jnp.sum((pair_rank[:rows] >= 0).astype(jnp.int32))
    pair_row = jnp.arange(2 * rows, dtype=jnp.int32)
    pair_rank = jnp.where(pair_rank >= 0, pair_rank + jnp.where(pair_row >= rows, count0, 0), -1)
    wanted = core * OWN + jnp.arange(OWN, dtype=jnp.int32)
    chosen = wanted[:, None] == pair_rank[None, :]
    picked = jnp.dot(chosen.astype(BF), pair, preferred_element_type=F32)
    token = zl * 2 * rows + jnp.sum(jnp.where(chosen, pair_row[None, :], 0), axis=1)
    position = picked[:, 513] * 128.0 + picked[:, 514]
    query = picked[:, :256].astype(BF).reshape(OWN, 2, HD).transpose(1, 0, 2).reshape(2 * OWN, HD)
    own_residual = picked[:, 256:512].astype(BF)
    far_residual = send(own_residual, EIGHT)

    kv_mine = jnp.concatenate(blocks)
    kv_theirs = send(kv_mine, CORE)
    key_row = jnp.arange(ZL * rows, dtype=jnp.int32)
    key_token = (zl - key_row // rows) * 2 * rows + key_row % rows
    query_token = jnp.concatenate([token, token])

    def scored(kv, offset):
        scores = lax.dot_general(query, kv[:, :HD], (((1,), (1,)), ((), ())), preferred_element_type=F32)
        at = key_token + offset
        visible = (at[None, :] <= query_token[:, None]) & (at >= 0)[None, :]
        return jnp.where(visible, scores * (1.0 / math.sqrt(HD)), -1e30)

    score_a = scored(kv_mine, core * rows)
    score_b = scored(kv_theirs, (1 - core) * rows)
    top = jnp.maximum(jnp.max(score_a, axis=1), jnp.max(score_b, axis=1))[:, None]
    prob_a, prob_b = jnp.exp(score_a - top), jnp.exp(score_b - top)
    total = jnp.sum(prob_a, axis=1) + jnp.sum(prob_b, axis=1)
    mixed = jnp.dot(prob_a.astype(BF), kv_mine[:, HD:], preferred_element_type=F32) + jnp.dot(
        prob_b.astype(BF), kv_theirs[:, HD:], preferred_element_type=F32
    )
    attended = (mixed / total[:, None]).astype(BF)
    attended = jnp.concatenate([attended[:OWN], attended[OWN:]], axis=1)

    both = jnp.concatenate([attended, send(attended, FOUR)])
    low = jnp.where(first, quad, quad_other)
    high = jnp.where(first, quad_other, quad)
    blocks_w = jnp.concatenate([low, high], axis=1)
    arranged = jnp.stack(
        [lax.dynamic_index_in_dim(blocks_w, (zl % 4) ^ k, 0, keepdims=False) for k in range(4)]
    ).reshape(NX * NY, 256, 256)
    terms = jnp.einsum("rk,ekn->ern", both, arranged, preferred_element_type=F32).astype(BF)
    summed = jnp.sum(plane_exchange(terms).reshape(NX * NY, 2 * OWN, 256).astype(F32), axis=0).astype(BF)
    near, far = summed[:OWN], summed[OWN:]
    from4, from8, from12 = send(far, FOUR), send(near, EIGHT), send(far, TWELVE)
    same = near.astype(F32) + from8.astype(F32)
    cross = from4.astype(F32) + from12.astype(F32)
    low_half = zl < 4
    first_half = jnp.where(low_half, same, cross)
    second_half = jnp.where(low_half, cross, same)
    hidden0 = (jnp.where(zh == 0, own_residual, far_residual).astype(F32) + first_half).astype(BF)
    hidden1 = (jnp.where(zh == 0, far_residual, own_residual).astype(F32) + second_half).astype(BF)
    hidden = jnp.concatenate([hidden0, hidden1], axis=1)

    wide = hidden.astype(F32)
    square = jnp.sum(wide * wide, axis=1, keepdims=True)
    square_high = square.astype(BF)
    square_low = (square - square_high.astype(F32)).astype(BF)
    parts = jnp.einsum(
        "rf,ecf->erc", hidden, gained.reshape(NX * NY, columns, -1), preferred_element_type=F32
    ).astype(BF)
    tail = jnp.pad(jnp.concatenate([square_high, square_low], axis=1), ((0, 0), (0, 128 - columns - 2)))
    message = jnp.concatenate([parts, jnp.broadcast_to(tail[None], (NX * NY,) + tail.shape)], axis=2)
    gathered = jnp.sum(plane_exchange(message).astype(F32), axis=0)
    square_total = gathered[:, columns] + gathered[:, columns + 1]
    cache_rows = gathered[:, :columns] * lax.rsqrt(square_total / D + EPS)[:, None]
    cache_rot = turn(cache_rows, position, tp * columns).astype(BF)

    own_hidden = jnp.where(zh == 0, hidden0, hidden1)
    done = jnp.concatenate([own_hidden, jnp.pad(cache_rot, ((0, 0), (0, 128 - columns)))], axis=1)
    done_other = send(done, CORE)
    kept = jnp.where(first, jnp.concatenate([done, done_other]), jnp.concatenate([done_other, done]))
    own_rank = jnp.where(rank >= 0, rank + jnp.where(first, 0, count0), -1)
    place = own_rank[:, None] == jnp.arange(PAIR_KEEP, dtype=jnp.int32)[None, :]
    output = jnp.dot(place.astype(BF), kept, preferred_element_type=F32).astype(BF)
    return output[:, :256], output[:, 256 : 256 + columns]


def solution(mesh):
    in_specs = (
        P("ctx", "tp"),
        P("ctx", "tp"),
        P("ctx", None),
        P("tp", "ctx"),
        P(),
        P(None, "tp"),
        P("ctx"),
        P("ctx"),
        P("ctx"),
    )
    out_specs = (P("ctx", "tp"), P("ctx", "tp"))
    return jax.shard_map(shards, mesh=mesh, in_specs=in_specs, out_specs=out_specs, check_vma=False)
```

```python
import math

import jax
import jax.numpy as jnp
from jax import lax
from jax.sharding import PartitionSpec as P

D = 8192
HQ = 64
KVH = 8
HD = 128
THETA = 1000000.0
EPS = 1e-06

ZL, CORES, ZH, NX, NY = 8, 2, 2, 4, 4
PAIR_KEEP = 320
OWN = PAIR_KEEP // 2
AXES = ("ctx", "tp")
BF = jnp.bfloat16
F32 = jnp.float32


def pairs(move):
    found = []
    for zl in range(ZL):
        for core in range(CORES):
            for zh in range(ZH):
                target = move(zh, zl, core)
                if target is None:
                    continue
                for plane in range(NX * NY):
                    source = (zl * CORES + core) * (ZH * NX * NY) + zh * NX * NY + plane
                    to = (target[1] * CORES + target[2]) * (ZH * NX * NY) + target[0] * NX * NY + plane
                    found.append((source, to))
    return found


CORE = pairs(lambda zh, zl, core: (zh, zl, 1 - core))
FOUR = pairs(lambda zh, zl, core: (zh, zl ^ 4, core))
EIGHT = pairs(lambda zh, zl, core: (1 - zh, zl, core))
TWELVE = pairs(lambda zh, zl, core: (1 - zh, zl ^ 4, core))
QUAD = [None] + [pairs(lambda zh, zl, core, k=k: (zh, zl ^ k, core)) for k in (1, 2, 3)]


def near(zl, k):
    return k < 4 or (k == 4 and zl >= 2)


BACK = [None] + [
    pairs(lambda zh, zl, core, k=k: (zh if near(zl, k) else 1 - zh, zl + k, core) if zl + k < ZL else None)
    for k in range(1, ZL)
]
PLANES = [[half * NX * NY + i for i in range(NX * NY)] for half in range(ZH)]
ALONG_Y = [[start * NY + y for y in range(NY)] for start in range(ZH * NX)]
ALONG_X = [[half * NX * NY + x * NY + y for x in range(NX)] for half in range(ZH) for y in range(NY)]


def send(x, table):
    return lax.ppermute(x, AXES, table)


def exchange(x, groups):
    return lax.all_to_all(x, "tp", 0, 0, tiled=True, axis_index_groups=groups)


def turn(cache_rows, position_ids, first_col):
    column = first_col + jnp.arange(cache_rows.shape[1], dtype=jnp.int32)
    within = column % (2 * HD)
    is_key = within < HD
    exponent = jnp.where(is_key, within - within % 2, 0).astype(F32) / HD
    frequency = jnp.power(F32(THETA), -exponent)
    angles = position_ids[:, None] * frequency[None, :]
    even = (column % 2 == 0)[None, :]
    other = jnp.where(even, -jnp.roll(cache_rows, -1, axis=1), jnp.roll(cache_rows, 1, axis=1))
    turned = cache_rows * jnp.cos(angles) + other * jnp.sin(angles)
    return jnp.where(is_key[None, :], turned, cache_rows)


def shards(
    residual, queries, keys_values, out_weight, norm_gain, cache_weight, positions, keep_rows, kept_count
):
    rows = residual.shape[0]
    ctx = lax.axis_index("ctx")
    tp = lax.axis_index("tp")
    zl, core = ctx // CORES, ctx % CORES
    zh, plane = tp // (NX * NY), tp % (NX * NY)
    first = core == 0

    local = jnp.arange(rows, dtype=jnp.int32)
    order = jnp.where(local < kept_count[0], local, -1)
    hits = keep_rows[:, None] == local[None, :]
    rank = jnp.sum(jnp.where(hits, order[:, None], 0), axis=0)
    meta = jnp.stack([rank, positions // 128, positions % 128], axis=1).astype(BF)
    meta = jnp.pad(meta, ((0, 0), (0, 125)))
    mine = jnp.concatenate([queries, residual, meta], axis=1)
    theirs = send(mine, CORE)

    head = zh * (KVH // ZH) + plane // NY
    far_head = (1 - zh) * (KVH // ZH) + plane // NY
    own_kv = lax.dynamic_slice_in_dim(keys_values, head * 2 * HD, 2 * HD, 1)
    far_kv = lax.dynamic_slice_in_dim(keys_values, far_head * 2 * HD, 2 * HD, 1)
    sent = {4: jnp.where(zl >= 2, own_kv, far_kv)}
    blocks = [own_kv] + [send(sent.get(k, own_kv if k < 4 else far_kv), BACK[k]) for k in range(1, ZL)]

    columns = cache_weight.shape[1]
    gained = (cache_weight.astype(F32) * norm_gain[:, None]).astype(BF)
    gained = gained.T.reshape(columns, ZH, NX * NY, D // (ZH * NX * NY)).transpose(2, 0, 1, 3)
    gained = exchange(gained.reshape(NX * NY, columns, -1), PLANES)

    kept_rows = lax.dynamic_slice_in_dim(out_weight, core * HD, HD, 0)
    given_rows = lax.dynamic_slice_in_dim(out_weight, (1 - core) * HD, HD, 0)
    taken_rows = send(given_rows, CORE)
    weight = jnp.concatenate(
        [jnp.where(first, kept_rows, taken_rows), jnp.where(first, taken_rows, kept_rows)], axis=1
    )
    weight = exchange(weight.reshape(HD, NY, 256).transpose(1, 0, 2), ALONG_Y).reshape(NY * HD, 256)

    pair = jnp.where(first, jnp.concatenate([mine, theirs]), jnp.concatenate([theirs, mine]))
    pair_rank = pair[:, 512].astype(jnp.int32)
    count0 = jnp.sum((pair_rank[:rows] >= 0).astype(jnp.int32))
    pair_row = jnp.arange(2 * rows, dtype=jnp.int32)
    pair_rank = jnp.where(pair_rank >= 0, pair_rank + jnp.where(pair_row >= rows, count0, 0), -1)
    wanted = core * OWN + jnp.arange(OWN, dtype=jnp.int32)
    chosen = wanted[:, None] == pair_rank[None, :]
    picked = jnp.dot(chosen.astype(BF), pair, preferred_element_type=F32)
    token = zl * 2 * rows + jnp.sum(jnp.where(chosen, pair_row[None, :], 0), axis=1)
    position = picked[:, 513] * 128.0 + picked[:, 514]
    query = picked[:, :256].astype(BF).reshape(OWN, 2, HD).transpose(1, 0, 2).reshape(2 * OWN, HD)
    own_residual = picked[:, 256:512].astype(BF)
    far_residual = send(own_residual, EIGHT)

    kv_mine = jnp.concatenate(blocks)
    kv_mine, weight, query, gained, far_residual = lax.optimization_barrier(
        (kv_mine, weight, query, gained, far_residual)
    )
    kv_theirs = send(kv_mine, CORE)
    quad = [weight] + [send(weight, QUAD[k]) for k in (1, 2, 3)]
    key_row = jnp.arange(ZL * rows, dtype=jnp.int32)
    key_token = (zl - key_row // rows) * 2 * rows + key_row % rows
    query_token = jnp.concatenate([token, token])

    def scored(kv, offset):
        scores = lax.dot_general(query, kv[:, :HD], (((1,), (1,)), ((), ())), preferred_element_type=F32)
        at = key_token + offset
        visible = (at[None, :] <= query_token[:, None]) & (at >= 0)[None, :]
        return jnp.where(visible, scores * (1.0 / math.sqrt(HD)), -1e30)

    score_a = scored(kv_mine, core * rows)
    score_b = scored(kv_theirs, (1 - core) * rows)
    top = jnp.maximum(jnp.max(score_a, axis=1), jnp.max(score_b, axis=1))[:, None]
    prob_a, prob_b = jnp.exp(score_a - top), jnp.exp(score_b - top)
    total = jnp.sum(prob_a, axis=1) + jnp.sum(prob_b, axis=1)
    mixed = jnp.dot(prob_a.astype(BF), kv_mine[:, HD:], preferred_element_type=F32) + jnp.dot(
        prob_b.astype(BF), kv_theirs[:, HD:], preferred_element_type=F32
    )
    attended = (mixed / total[:, None]).astype(BF)
    attended = attended.reshape(2, OWN, HD)

    both = jnp.stack([attended, send(attended, FOUR)])
    both, quad = lax.optimization_barrier((both, quad))
    heads = exchange(jnp.broadcast_to(both[None], (NY,) + both.shape).reshape(NY * 2, 2, OWN, HD), ALONG_Y)
    heads = heads.reshape(NY, 2, 2, OWN, HD).transpose(1, 3, 2, 0, 4).reshape(2 * OWN, 2 * NY * HD)
    quad = jnp.stack(quad)
    quad = jnp.stack([lax.dynamic_index_in_dim(quad, (zl % 4) ^ k, 0, keepdims=False) for k in range(NX)])
    quad_other = send(quad, CORE)
    full = jnp.concatenate(
        [jnp.where(first, quad, quad_other), jnp.where(first, quad_other, quad)], axis=1
    )
    terms = jnp.einsum("rk,ekn->ern", heads, full, preferred_element_type=F32).astype(BF)
    summed = jnp.sum(exchange(terms, ALONG_X).reshape(NX, 2 * OWN, 256).astype(F32), axis=0).astype(BF)
    here, away = summed[:OWN], summed[OWN:]
    from4, from8, from12 = send(away, FOUR), send(here, EIGHT), send(away, TWELVE)
    same = here.astype(F32) + from8.astype(F32)
    cross = from4.astype(F32) + from12.astype(F32)
    low_half = zl < 4
    first_half = jnp.where(low_half, same, cross)
    second_half = jnp.where(low_half, cross, same)
    hidden0 = (jnp.where(zh == 0, own_residual, far_residual).astype(F32) + first_half).astype(BF)
    hidden1 = (jnp.where(zh == 0, far_residual, own_residual).astype(F32) + second_half).astype(BF)
    hidden = jnp.concatenate([hidden0, hidden1], axis=1)

    wide = hidden.astype(F32)
    square = jnp.sum(wide * wide, axis=1, keepdims=True)
    square_high = square.astype(BF)
    square_low = (square - square_high.astype(F32)).astype(BF)
    parts = jnp.einsum(
        "rf,ecf->erc", hidden, gained.reshape(NX * NY, columns, -1), preferred_element_type=F32
    ).astype(BF)
    tail = jnp.pad(jnp.concatenate([square_high, square_low], axis=1), ((0, 0), (0, 128 - columns - 2)))
    message = jnp.concatenate([parts, jnp.broadcast_to(tail[None], (NX * NY,) + tail.shape)], axis=2)
    gathered = jnp.sum(exchange(message, PLANES).astype(F32), axis=0)
    square_total = gathered[:, columns] + gathered[:, columns + 1]
    cache_rows = gathered[:, :columns] * lax.rsqrt(square_total / D + EPS)[:, None]
    cache_rot = turn(cache_rows, position, tp * columns).astype(BF)

    own_hidden = jnp.where(zh == 0, hidden0, hidden1)
    done = jnp.concatenate([own_hidden, jnp.pad(cache_rot, ((0, 0), (0, 128 - columns)))], axis=1)
    done_other = send(done, CORE)
    kept = jnp.where(first, jnp.concatenate([done, done_other]), jnp.concatenate([done_other, done]))
    own_rank = jnp.where(rank >= 0, rank + jnp.where(first, 0, count0), -1)
    place = own_rank[:, None] == jnp.arange(PAIR_KEEP, dtype=jnp.int32)[None, :]
    output = jnp.dot(place.astype(BF), kept, preferred_element_type=F32).astype(BF)
    return output[:, :256], output[:, 256 : 256 + columns]


def solution(mesh):
    in_specs = (
        P("ctx", "tp"),
        P("ctx", "tp"),
        P("ctx", None),
        P("tp", "ctx"),
        P(),
        P(None, "tp"),
        P("ctx"),
        P("ctx"),
        P("ctx"),
    )
    out_specs = (P("ctx", "tp"), P("ctx", "tp"))
    return jax.shard_map(shards, mesh=mesh, in_specs=in_specs, out_specs=out_specs, check_vma=False)
```

```python
import itertools
import math

import jax
import jax.numpy as jnp
from jax import lax
from jax.sharding import PartitionSpec as P

D = 8192
HQ = 64
KVH = 8
HD = 128
THETA = 1000000.0
EPS = 1e-06

ZL, CORES, ZH, NX, NY = 8, 2, 2, 4, 4
PAIR_KEEP = 320
OWN = PAIR_KEEP // 2
AXES = ("ctx", "tp")
BF = jnp.bfloat16
F32 = jnp.float32


def pairs(**moves):
    names = ("zh", "zl", "core", "x", "y")
    found = []
    for source in itertools.product(range(ZH), range(ZL), range(CORES), range(NX), range(NY)):
        at = dict(zip(names, source))
        target = {**at, **{name: move(at) for name, move in moves.items()}}
        if target["zl"] < ZL:
            found.append((place(*source), place(**target)))
    return found


def place(zh, zl, core, x, y):
    return (zl * CORES + core) * (ZH * NX * NY) + (zh * NX + x) * NY + y


CORE = pairs(core=lambda at: 1 - at["core"])
FOUR = pairs(zl=lambda at: at["zl"] ^ 4)
NEXT_X = [None] + [pairs(x=lambda at, k=k: (at["x"] + k) % NX) for k in (1, 2, 3)]
NEXT_Y = [None] + [pairs(y=lambda at, k=k: (at["y"] + k) % NY) for k in (1, 2, 3)]
PLANES = [[half * NX * NY + i for i in range(NX * NY)] for half in range(ZH)]
ALONG_Y = [[start * NY + y for y in range(NY)] for start in range(ZH * NX)]
ALONG_X = [[half * NX * NY + x * NY + y for x in range(NX)] for half in range(ZH) for y in range(NY)]
QUADS = [
    [place(zh, quad * 4 + low, core, x, y) for low in range(4) for y in range(NY)]
    for zh in range(ZH)
    for quad in range(2)
    for core in range(CORES)
    for x in range(NX)
]
SETS = [
    [place(zh, zl, core, x, y) for zh in range(ZH) for zl in (low, low + 4)]
    for low in range(4)
    for core in range(CORES)
    for x in range(NX)
    for y in range(NY)
]


def near(zl, k):
    return k < 4 or (k == 4 and zl >= 2)


BACK = [None] + [
    pairs(
        zh=lambda at, k=k: at["zh"] if near(at["zl"], k) else 1 - at["zh"],
        zl=lambda at, k=k: at["zl"] + k,
    )
    for k in range(1, ZL)
]


def send(x, table):
    return lax.ppermute(x, AXES, table)


def exchange(x, groups, axes="tp"):
    return lax.all_to_all(x, axes, 0, 0, tiled=True, axis_index_groups=groups)


def swap(x, me, tables):
    count = len(tables)
    out = [lax.dynamic_index_in_dim(x, (me + k) % count, 0, keepdims=False) for k in range(count)]
    got = jnp.stack([out[0]] + [send(out[k], tables[k]) for k in range(1, count)])
    return jnp.stack(
        [lax.dynamic_index_in_dim(got, (me - k) % count, 0, keepdims=False) for k in range(count)]
    )


def turn(cache_rows, position_ids, first_col):
    column = first_col + jnp.arange(cache_rows.shape[1], dtype=jnp.int32)
    within = column % (2 * HD)
    is_key = within < HD
    exponent = jnp.where(is_key, within - within % 2, 0).astype(F32) / HD
    frequency = jnp.power(F32(THETA), -exponent)
    angles = position_ids[:, None] * frequency[None, :]
    even = (column % 2 == 0)[None, :]
    other = jnp.where(even, -jnp.roll(cache_rows, -1, axis=1), jnp.roll(cache_rows, 1, axis=1))
    turned = cache_rows * jnp.cos(angles) + other * jnp.sin(angles)
    return jnp.where(is_key[None, :], turned, cache_rows)


def shards(
    residual, queries, keys_values, out_weight, norm_gain, cache_weight, positions, keep_rows, kept_count
):
    rows = residual.shape[0]
    ctx = lax.axis_index("ctx")
    tp = lax.axis_index("tp")
    zl, core = ctx // CORES, ctx % CORES
    zh, plane = tp // (NX * NY), tp % (NX * NY)
    x, y = plane // NY, plane % NY
    first = core == 0

    local = jnp.arange(rows, dtype=jnp.int32)
    order = jnp.where(local < kept_count[0], local, -1)
    hits = keep_rows[:, None] == local[None, :]
    rank = jnp.sum(jnp.where(hits, order[:, None], 0), axis=0)
    meta = jnp.stack([rank, positions // 128, positions % 128], axis=1).astype(BF)
    meta = jnp.pad(meta, ((0, 0), (0, 125)))
    mine = jnp.concatenate([queries, residual, meta], axis=1)

    head = zh * (KVH // ZH) + plane // NY
    far_head = (1 - zh) * (KVH // ZH) + plane // NY
    own_kv = lax.dynamic_slice_in_dim(keys_values, head * 2 * HD, 2 * HD, 1)
    far_kv = lax.dynamic_slice_in_dim(keys_values, far_head * 2 * HD, 2 * HD, 1)
    sent = {4: jnp.where(zl >= 2, own_kv, far_kv)}
    blocks = [own_kv] + [send(sent.get(k, own_kv if k < 4 else far_kv), BACK[k]) for k in range(1, ZL)]

    kept_rows = lax.dynamic_slice_in_dim(out_weight, core * HD, HD, 0)
    given_rows = lax.dynamic_slice_in_dim(out_weight, (1 - core) * HD, HD, 0)
    taken_rows = send(given_rows, CORE)
    weight = jnp.concatenate(
        [jnp.where(first, kept_rows, taken_rows), jnp.where(first, taken_rows, kept_rows)], axis=1
    )
    weight = weight.reshape(HD, NY, 256).transpose(1, 0, 2)
    weight = jnp.broadcast_to(weight[None], (4,) + weight.shape).reshape(4 * NY, HD, 256)
    weight, mine = lax.optimization_barrier((weight, mine))
    quad = exchange(weight, QUADS, AXES).reshape(NX, NY * HD, 256)
    theirs = send(mine, CORE)

    pair = jnp.where(first, jnp.concatenate([mine, theirs]), jnp.concatenate([theirs, mine]))
    pair_rank = pair[:, 512].astype(jnp.int32)
    count0 = jnp.sum((pair_rank[:rows] >= 0).astype(jnp.int32))
    pair_row = jnp.arange(2 * rows, dtype=jnp.int32)
    pair_rank = jnp.where(pair_rank >= 0, pair_rank + jnp.where(pair_row >= rows, count0, 0), -1)
    wanted = core * OWN + jnp.arange(OWN, dtype=jnp.int32)
    chosen = wanted[:, None] == pair_rank[None, :]
    picked = jnp.dot(chosen.astype(BF), pair, preferred_element_type=F32)
    token = zl * 2 * rows + jnp.sum(jnp.where(chosen, pair_row[None, :], 0), axis=1)
    position = picked[:, 513] * 128.0 + picked[:, 514]
    query = picked[:, :256].astype(BF).reshape(OWN, 2, HD).transpose(1, 0, 2).reshape(2 * OWN, HD)
    own_residual = picked[:, 256:512].astype(BF)

    kv_mine = jnp.concatenate(lax.optimization_barrier(blocks))
    kv_theirs = send(kv_mine, CORE)
    key_row = jnp.arange(ZL * rows, dtype=jnp.int32)
    key_token = (zl - key_row // rows) * 2 * rows + key_row % rows
    query_token = jnp.concatenate([token, token])

    def scored(kv, offset):
        scores = lax.dot_general(query, kv[:, :HD], (((1,), (1,)), ((), ())), preferred_element_type=F32)
        at = key_token + offset
        visible = (at[None, :] <= query_token[:, None]) & (at >= 0)[None, :]
        return jnp.where(visible, scores * (1.0 / math.sqrt(HD)), -1e30)

    score_a = scored(kv_mine, core * rows)
    score_b = scored(kv_theirs, (1 - core) * rows)
    top = jnp.maximum(jnp.max(score_a, axis=1), jnp.max(score_b, axis=1))[:, None]
    prob_a, prob_b = jnp.exp(score_a - top), jnp.exp(score_b - top)
    total = jnp.sum(prob_a, axis=1) + jnp.sum(prob_b, axis=1)
    mixed = jnp.dot(prob_a.astype(BF), kv_mine[:, HD:], preferred_element_type=F32) + jnp.dot(
        prob_b.astype(BF), kv_theirs[:, HD:], preferred_element_type=F32
    )
    attended = (mixed / total[:, None]).astype(BF)

    attended = attended.reshape(2, OWN, HD)
    attended = jnp.where(first, attended, attended[::-1])
    paired_residual = own_residual.reshape(OWN, 2, HD).transpose(1, 0, 2)
    partner = send(jnp.concatenate([attended, paired_residual]), FOUR)
    partner_residual = jnp.concatenate([partner[2], partner[3]], axis=1)
    partner = partner[:2]
    low = zl < 4
    both = jnp.concatenate([jnp.where(low, attended, partner), jnp.where(low, partner, attended)], axis=1)
    both, cache_weight, quad = lax.optimization_barrier((both, cache_weight, quad))
    quad_other = send(quad, CORE)
    cache_weight, quad_other = lax.optimization_barrier((cache_weight, quad_other))

    columns = cache_weight.shape[1]
    part = D // ZH
    gained = lax.dynamic_slice_in_dim(cache_weight, core * part, part, 0).astype(F32)
    gained = (gained * lax.dynamic_slice_in_dim(norm_gain, core * part, part, 0)[:, None]).astype(BF)
    gained = gained.T.reshape(columns, NX, NY, 256).transpose(1, 2, 0, 3)
    gained = swap(gained, x, NEXT_X).transpose(1, 0, 2, 3)

    heads = exchange(jnp.broadcast_to(both[None], (NY,) + both.shape), ALONG_Y)
    gained = swap(gained, y, NEXT_Y).transpose(1, 0, 2, 3).reshape(NX * NY, columns, 256)
    gained_other = send(gained, CORE)
    terms = 0.0
    for k, block in enumerate((quad, quad_other)):
        side = jnp.concatenate([heads[j, k] for j in range(NY)], axis=1)
        terms = terms + jnp.einsum("rk,ekn->ern", side, block, preferred_element_type=F32)
    terms = terms.astype(BF)
    summed = jnp.sum(exchange(terms, ALONG_X).reshape(NX, 2 * OWN, 256).astype(F32), axis=0)
    rest = jnp.concatenate(
        [jnp.where(low, own_residual, partner_residual), jnp.where(low, partner_residual, own_residual)]
    )
    holds = (zh == 0) == low
    summed = jnp.where(holds, summed + rest.astype(F32), summed).astype(BF).reshape(2, OWN, 256)
    halves = exchange(jnp.concatenate([summed, summed]), SETS, AXES).astype(F32)
    hidden0 = (halves[0] + halves[2]).astype(BF)
    hidden1 = (halves[1] + halves[3]).astype(BF)

    wide0, wide1 = hidden0.astype(F32), hidden1.astype(F32)
    square = jnp.sum(wide0 * wide0 + wide1 * wide1, axis=1, keepdims=True)
    square_high = square.astype(BF)
    square_low = (square - square_high.astype(F32)).astype(BF)
    parts = jnp.einsum(
        "rf,ecf->erc", jnp.where(first, hidden0, hidden1), gained, preferred_element_type=F32
    ) + jnp.einsum(
        "rf,ecf->erc", jnp.where(first, hidden1, hidden0), gained_other, preferred_element_type=F32
    )
    parts = parts.astype(BF)
    tail = jnp.pad(jnp.concatenate([square_high, square_low], axis=1), ((0, 0), (0, 128 - columns - 2)))
    message = jnp.concatenate([parts, jnp.broadcast_to(tail[None], (NX * NY,) + tail.shape)], axis=2)
    gathered = jnp.sum(exchange(message, PLANES).astype(F32), axis=0)
    square_total = gathered[:, columns] + gathered[:, columns + 1]
    cache_rows = gathered[:, :columns] * lax.rsqrt(square_total / D + EPS)[:, None]
    cache_rot = turn(cache_rows, position, tp * columns).astype(BF)

    own_hidden = jnp.where(zh == 0, hidden0, hidden1)
    done = jnp.concatenate([own_hidden, jnp.pad(cache_rot, ((0, 0), (0, 128 - columns)))], axis=1)
    done_other = send(done, CORE)
    kept = jnp.where(first, jnp.concatenate([done, done_other]), jnp.concatenate([done_other, done]))
    own_rank = jnp.where(rank >= 0, rank + jnp.where(first, 0, count0), -1)
    put = own_rank[:, None] == jnp.arange(PAIR_KEEP, dtype=jnp.int32)[None, :]
    output = jnp.dot(put.astype(BF), kept, preferred_element_type=F32).astype(BF)
    return output[:, :256], output[:, 256 : 256 + columns]


def solution(mesh):
    in_specs = (
        P("ctx", "tp"),
        P("ctx", "tp"),
        P("ctx", None),
        P("tp", "ctx"),
        P(),
        P(None, "tp"),
        P("ctx"),
        P("ctx"),
        P("ctx"),
    )
    out_specs = (P("ctx", "tp"), P("ctx", "tp"))
    return jax.shard_map(shards, mesh=mesh, in_specs=in_specs, out_specs=out_specs, check_vma=False)
```

```python
import functools
import itertools
import math

import jax
import jax.numpy as jnp
from jax import lax
from jax.experimental import pallas as pl
from jax.experimental.pallas import tpu as pltpu
from jax.sharding import PartitionSpec as P

D = 8192
HQ = 64
KVH = 8
HD = 128
THETA = 1000000.0
EPS = 1e-06

ZL, CORES, ZH, NX, NY = 8, 2, 2, 4, 4
PAIR_KEEP = 320
OWN = PAIR_KEEP // 2
AXES = ("ctx", "tp")
BF = jnp.bfloat16
F32 = jnp.float32


def pairs(**moves):
    names = ("zh", "zl", "core", "x", "y")
    found = []
    for source in itertools.product(range(ZH), range(ZL), range(CORES), range(NX), range(NY)):
        at = dict(zip(names, source))
        target = {**at, **{name: move(at) for name, move in moves.items()}}
        if target["zl"] < ZL:
            found.append((place(*source), place(**target)))
    return found


def place(zh, zl, core, x, y):
    return (zl * CORES + core) * (ZH * NX * NY) + (zh * NX + x) * NY + y


CORE = pairs(core=lambda at: 1 - at["core"])
FOUR = pairs(zl=lambda at: at["zl"] ^ 4)
NEXT_X = [None] + [pairs(x=lambda at, k=k: (at["x"] + k) % NX) for k in (1, 2, 3)]
NEXT_Y = [None] + [pairs(y=lambda at, k=k: (at["y"] + k) % NY) for k in (1, 2, 3)]
PLANES = [[half * NX * NY + i for i in range(NX * NY)] for half in range(ZH)]
ALONG_Y = [[start * NY + y for y in range(NY)] for start in range(ZH * NX)]
ALONG_X = [[half * NX * NY + x * NY + y for x in range(NX)] for half in range(ZH) for y in range(NY)]
QUADS = [
    [place(zh, quad * 4 + low, core, x, y) for low in range(4) for y in range(NY)]
    for zh in range(ZH)
    for quad in range(2)
    for core in range(CORES)
    for x in range(NX)
]
SETS = [
    [place(zh, zl, core, x, y) for zh in range(ZH) for zl in (low, low + 4)]
    for low in range(4)
    for core in range(CORES)
    for x in range(NX)
    for y in range(NY)
]


def near(zl, k):
    return k < 4 or (k == 4 and zl >= 2)


BACK = [None] + [
    pairs(
        zh=lambda at, k=k: at["zh"] if near(at["zl"], k) else 1 - at["zh"],
        zl=lambda at, k=k: at["zl"] + k,
    )
    for k in range(1, ZL)
]


def send(x, table):
    return lax.ppermute(x, AXES, table)


def exchange(x, groups, axes="tp"):
    return lax.all_to_all(x, axes, 0, 0, tiled=True, axis_index_groups=groups)


def swap(x, me, tables):
    count = len(tables)
    out = [lax.dynamic_index_in_dim(x, (me + k) % count, 0, keepdims=False) for k in range(count)]
    got = jnp.stack([out[0]] + [send(out[k], tables[k]) for k in range(1, count)])
    return jnp.stack(
        [lax.dynamic_index_in_dim(got, (me - k) % count, 0, keepdims=False) for k in range(count)]
    )


def attend_kernel(place_ref, query_ref, token_ref, *refs):
    own_ref, quarters = refs[0], refs[1 : 1 + NY]
    out_ref, scores_ref, top_ref, total_ref, sum_ref = refs[1 + NY :]
    zl, core = place_ref[0], place_ref[1]
    scale = 1.0 / math.sqrt(HD)
    groups = [pl.ds(group * OWN, OWN) for group in range(4)]
    top_ref[...] = jnp.full(top_ref.shape, -1e29, F32)
    total_ref[...] = jnp.zeros(total_ref.shape, F32)
    sum_ref[...] = jnp.zeros(sum_ref.shape, F32)

    def block(k, columns):
        if k == 0:
            return own_ref[:, columns]
        return jnp.concatenate([quarter[k - 1, :, columns] for quarter in quarters])

    def score(k):
        key = block(k, pl.ds(0, HD))
        for here in groups:
            scores = lax.dot_general(
                query_ref[here, :], key, (((1,), (1,)), ((), ())), preferred_element_type=F32
            )
            if k == 0:
                at = core * scores.shape[1] + lax.broadcasted_iota(jnp.int32, scores.shape, 1)
                scores = jnp.where(at <= token_ref[here, :], scores, -1e30)
            scores_ref[k, here, :] = scores
            top = jnp.maximum(scores[:, :HD], scores[:, HD:])
            top_ref[here, :] = jnp.maximum(top_ref[here, :], top)

    def add(k):
        value = block(k, pl.ds(HD, HD))
        for here in groups:
            top = top_ref[here, :]
            scores = scores_ref[k, here, :]
            low, high = jnp.exp((scores[:, :HD] - top) * scale), jnp.exp((scores[:, HD:] - top) * scale)
            total_ref[here, :] = total_ref[here, :] + (low + high)
            probs = jnp.concatenate([low.astype(BF), high.astype(BF)], axis=1)
            sum_ref[here, :] = sum_ref[here, :] + jnp.dot(probs, value, preferred_element_type=F32)

    score(0)
    for k in range(1, ZL):
        pl.when(zl >= k)(functools.partial(score, k))
    for here in groups:
        top = jnp.max(top_ref[here, :], axis=1, keepdims=True)
        top_ref[here, :] = jnp.broadcast_to(top, (OWN, HD))
    add(0)
    for k in range(1, ZL):
        pl.when(zl >= k)(functools.partial(add, k))

    lane = lax.broadcasted_iota(jnp.int32, (OWN, HD), 1)
    for side in range(2):
        for head in range(2):
            here = groups[side * 2 + head]
            total = jnp.sum(total_ref[here, :], axis=1, keepdims=True)
            out_ref[side, head] = sum_ref[here, :]
            out_ref[side, 2 + head] = jnp.where(lane == 0, top_ref[here, :] * scale, total)


def attend(where, query, token, own, quarters):
    whole = pl.BlockSpec(memory_space=pltpu.VMEM)
    rows = query.shape[0]
    return pl.pallas_call(
        attend_kernel,
        out_shape=jax.ShapeDtypeStruct((2, 4, OWN, HD), F32),
        in_specs=[pl.BlockSpec(memory_space=pltpu.SMEM)] + [whole] * (3 + len(quarters)),
        out_specs=whole,
        scratch_shapes=[
            pltpu.VMEM((ZL, rows, own.shape[0]), F32),
            pltpu.VMEM((rows, HD), F32),
            pltpu.VMEM((rows, HD), F32),
            pltpu.VMEM((rows, HD), F32),
        ],
        compiler_params=pltpu.CompilerParams(vmem_limit_bytes=32 * 1024 * 1024),
    )(where, query, token, own, *quarters)


def turn(cache_rows, position_ids, first_col):
    column = first_col + jnp.arange(cache_rows.shape[1], dtype=jnp.int32)
    within = column % (2 * HD)
    is_key = within < HD
    exponent = jnp.where(is_key, within - within % 2, 0).astype(F32) / HD
    frequency = jnp.power(F32(THETA), -exponent)
    angles = position_ids[:, None] * frequency[None, :]
    even = (column % 2 == 0)[None, :]
    other = jnp.where(even, -jnp.roll(cache_rows, -1, axis=1), jnp.roll(cache_rows, 1, axis=1))
    turned = cache_rows * jnp.cos(angles) + other * jnp.sin(angles)
    return jnp.where(is_key[None, :], turned, cache_rows)


def shards(
    residual, queries, keys_values, out_weight, norm_gain, cache_weight, positions, keep_rows, kept_count
):
    rows = residual.shape[0]
    ctx = lax.axis_index("ctx")
    tp = lax.axis_index("tp")
    zl, core = ctx // CORES, ctx % CORES
    zh, plane = tp // (NX * NY), tp % (NX * NY)
    x, y = plane // NY, plane % NY
    first = core == 0

    local = jnp.arange(rows, dtype=jnp.int32)
    order = jnp.where(local < kept_count[0], local, -1)
    hits = keep_rows[:, None] == local[None, :]
    rank = jnp.sum(jnp.where(hits, order[:, None], 0), axis=0)
    meta = jnp.stack([rank, positions // 128, positions % 128], axis=1).astype(BF)
    meta = jnp.pad(meta, ((0, 0), (0, 125)))
    mine = jnp.concatenate([queries, residual, meta], axis=1)

    head = zh * (KVH // ZH) + plane // NY
    far_head = (1 - zh) * (KVH // ZH) + plane // NY
    own_kv = lax.dynamic_slice_in_dim(keys_values, head * 2 * HD, 2 * HD, 1)
    far_kv = lax.dynamic_slice_in_dim(keys_values, far_head * 2 * HD, 2 * HD, 1)
    quarter = rows // NY
    near_kv = lax.dynamic_slice_in_dim(own_kv, y * quarter, quarter, 0)
    far_kv = lax.dynamic_slice_in_dim(far_kv, y * quarter, quarter, 0)
    sent = {4: jnp.where(zl >= 2, near_kv, far_kv)}
    blocks = [send(sent.get(k, near_kv if k < 4 else far_kv), BACK[k]) for k in range(1, ZL)]
    quarters = jnp.stack(blocks)
    quarters = [quarters] + [send(quarters, NEXT_Y[k]) for k in (1, 2, 3)]

    kept_rows = lax.dynamic_slice_in_dim(out_weight, core * HD, HD, 0)
    given_rows = lax.dynamic_slice_in_dim(out_weight, (1 - core) * HD, HD, 0)
    taken_rows = send(given_rows, CORE)
    weight = jnp.concatenate(
        [jnp.where(first, kept_rows, taken_rows), jnp.where(first, taken_rows, kept_rows)], axis=1
    )
    weight = weight.reshape(HD, NY, 256).transpose(1, 0, 2)
    weight = jnp.broadcast_to(weight[None], (4,) + weight.shape).reshape(4 * NY, HD, 256)
    theirs = send(mine, CORE)
    weight, theirs, _ = lax.optimization_barrier((weight, theirs, blocks))
    quad = exchange(weight, QUADS, AXES).reshape(NX, NY * HD, 256)

    pair = jnp.where(first, jnp.concatenate([mine, theirs]), jnp.concatenate([theirs, mine]))
    pair_rank = pair[:, 512].astype(jnp.int32)
    count0 = jnp.sum((pair_rank[:rows] >= 0).astype(jnp.int32))
    pair_row = jnp.arange(2 * rows, dtype=jnp.int32)
    pair_rank = jnp.where(pair_rank >= 0, pair_rank + jnp.where(pair_row >= rows, count0, 0), -1)
    wanted = jnp.arange(OWN, dtype=jnp.int32)
    wanted = jnp.concatenate([core * OWN + wanted, (1 - core) * OWN + wanted])
    chosen = wanted[:, None] == pair_rank[None, :]
    picked = jnp.dot(chosen.astype(BF), pair, preferred_element_type=F32)
    token = jnp.sum(jnp.where(chosen, pair_row[None, :], 0), axis=1)
    position = picked[:OWN, 513] * 128.0 + picked[:OWN, 514]
    query = picked[:, :256].astype(BF).reshape(2, OWN, 2, HD).transpose(0, 2, 1, 3).reshape(4 * OWN, HD)
    own_residual = picked[:OWN, 256:512].astype(BF)

    token = jnp.broadcast_to(token.reshape(2, 1, OWN), (2, 2, OWN)).reshape(4 * OWN, 1)
    parts = attend(jnp.stack([zl, core]).astype(jnp.int32), query, token, own_kv, quarters)
    kept_part, taken_part = parts[0], send(parts[1], CORE)
    top_a, top_b = kept_part[2:, :, :1], taken_part[2:, :, :1]
    top = jnp.maximum(top_a, top_b)
    fade_a, fade_b = jnp.exp(top_a - top), jnp.exp(top_b - top)
    total = kept_part[2:, :, 1:2] * fade_a + taken_part[2:, :, 1:2] * fade_b
    attended = ((kept_part[:2] * fade_a + taken_part[:2] * fade_b) / total).astype(BF)

    attended = jnp.where(first, attended, attended[::-1])
    paired_residual = own_residual.reshape(OWN, 2, HD).transpose(1, 0, 2)
    partner = send(jnp.concatenate([attended, paired_residual]), FOUR)
    partner_residual = jnp.concatenate([partner[2], partner[3]], axis=1)
    partner = partner[:2]
    low = zl < 4
    both = jnp.concatenate([jnp.where(low, attended, partner), jnp.where(low, partner, attended)], axis=1)
    both, cache_weight, quad = lax.optimization_barrier((both, cache_weight, quad))
    quad_other = send(quad, CORE)
    cache_weight, quad_other = lax.optimization_barrier((cache_weight, quad_other))

    columns = cache_weight.shape[1]
    part = D // ZH
    gained = lax.dynamic_slice_in_dim(cache_weight, core * part, part, 0).astype(F32)
    gained = (gained * lax.dynamic_slice_in_dim(norm_gain, core * part, part, 0)[:, None]).astype(BF)
    gained = gained.T.reshape(columns, NX, NY, 256).transpose(1, 2, 0, 3)
    gained = swap(gained, x, NEXT_X).transpose(1, 0, 2, 3)

    heads = exchange(jnp.broadcast_to(both[None], (NY,) + both.shape), ALONG_Y)
    gained = swap(gained, y, NEXT_Y).transpose(1, 0, 2, 3).reshape(NX * NY, columns, 256)
    gained_other = send(gained, CORE)
    terms = 0.0
    for k, block in enumerate((quad, quad_other)):
        side = jnp.concatenate([heads[j, k] for j in range(NY)], axis=1)
        terms = terms + jnp.einsum("rk,ekn->ern", side, block, preferred_element_type=F32)
    terms = terms.astype(BF)
    summed = jnp.sum(exchange(terms, ALONG_X).reshape(NX, 2 * OWN, 256).astype(F32), axis=0)
    rest = jnp.concatenate(
        [jnp.where(low, own_residual, partner_residual), jnp.where(low, partner_residual, own_residual)]
    )
    holds = (zh == 0) == low
    summed = jnp.where(holds, summed + rest.astype(F32), summed).astype(BF).reshape(2, OWN, 256)
    halves = exchange(jnp.concatenate([summed, summed]), SETS, AXES).astype(F32)
    hidden0 = (halves[0] + halves[2]).astype(BF)
    hidden1 = (halves[1] + halves[3]).astype(BF)

    wide0, wide1 = hidden0.astype(F32), hidden1.astype(F32)
    square = jnp.sum(wide0 * wide0 + wide1 * wide1, axis=1, keepdims=True)
    square_high = square.astype(BF)
    square_low = (square - square_high.astype(F32)).astype(BF)
    parts = jnp.einsum(
        "rf,ecf->erc", jnp.where(first, hidden0, hidden1), gained, preferred_element_type=F32
    ) + jnp.einsum(
        "rf,ecf->erc", jnp.where(first, hidden1, hidden0), gained_other, preferred_element_type=F32
    )
    parts = parts.astype(BF)
    tail = jnp.pad(jnp.concatenate([square_high, square_low], axis=1), ((0, 0), (0, 128 - columns - 2)))
    message = jnp.concatenate([parts, jnp.broadcast_to(tail[None], (NX * NY,) + tail.shape)], axis=2)
    gathered = jnp.sum(exchange(message, PLANES).astype(F32), axis=0)
    square_total = gathered[:, columns] + gathered[:, columns + 1]
    cache_rows = gathered[:, :columns] * lax.rsqrt(square_total / D + EPS)[:, None]
    cache_rot = turn(cache_rows, position, tp * columns).astype(BF)

    own_hidden = jnp.where(zh == 0, hidden0, hidden1)
    done = jnp.concatenate([own_hidden, jnp.pad(cache_rot, ((0, 0), (0, 128 - columns)))], axis=1)
    done_other = send(done, CORE)
    kept = jnp.where(first, jnp.concatenate([done, done_other]), jnp.concatenate([done_other, done]))
    own_rank = jnp.where(rank >= 0, rank + jnp.where(first, 0, count0), -1)
    put = own_rank[:, None] == jnp.arange(PAIR_KEEP, dtype=jnp.int32)[None, :]
    output = jnp.dot(put.astype(BF), kept, preferred_element_type=F32).astype(BF)
    return output[:, :256], output[:, 256 : 256 + columns]


def solution(mesh):
    in_specs = (
        P("ctx", "tp"),
        P("ctx", "tp"),
        P("ctx", None),
        P("tp", "ctx"),
        P(),
        P(None, "tp"),
        P("ctx"),
        P("ctx"),
        P("ctx"),
    )
    out_specs = (P("ctx", "tp"), P("ctx", "tp"))
    return jax.shard_map(shards, mesh=mesh, in_specs=in_specs, out_specs=out_specs, check_vma=False)
```

```python
import itertools
import math

import jax
import jax.numpy as jnp
from jax import lax
from jax.sharding import PartitionSpec as P

D = 8192
HQ = 64
KVH = 8
HD = 128
THETA = 1000000.0
EPS = 1e-06

ZL, CORES, ZH, NX, NY = 8, 2, 2, 4, 4
PAIR_KEEP = 320
OWN = PAIR_KEEP // 2
AXES = ("ctx", "tp")
BF = jnp.bfloat16
F32 = jnp.float32


def pairs(**moves):
    names = ("zh", "zl", "core", "x", "y")
    found = []
    for source in itertools.product(range(ZH), range(ZL), range(CORES), range(NX), range(NY)):
        at = dict(zip(names, source))
        target = {**at, **{name: move(at) for name, move in moves.items()}}
        if target["zl"] < ZL:
            found.append((place(*source), place(**target)))
    return found


def place(zh, zl, core, x, y):
    return (zl * CORES + core) * (ZH * NX * NY) + (zh * NX + x) * NY + y


CORE = pairs(core=lambda at: 1 - at["core"])
FOUR = pairs(zl=lambda at: at["zl"] ^ 4)
NEXT_X = [None] + [pairs(x=lambda at, k=k: (at["x"] + k) % NX) for k in (1, 2, 3)]
NEXT_Y = [None] + [pairs(y=lambda at, k=k: (at["y"] + k) % NY) for k in (1, 2, 3)]
PLANES = [[half * NX * NY + i for i in range(NX * NY)] for half in range(ZH)]
ALONG_Y = [[start * NY + y for y in range(NY)] for start in range(ZH * NX)]
ALONG_X = [[half * NX * NY + x * NY + y for x in range(NX)] for half in range(ZH) for y in range(NY)]
QUADS = [
    [place(zh, quad * 4 + low, core, x, y) for low in range(4) for y in range(NY)]
    for zh in range(ZH)
    for quad in range(2)
    for core in range(CORES)
    for x in range(NX)
]
SETS = [
    [place(zh, zl, core, x, y) for zh in range(ZH) for zl in (low, low + 4)]
    for low in range(4)
    for core in range(CORES)
    for x in range(NX)
    for y in range(NY)
]


def near(zl, k):
    return k < 4 or (k == 4 and zl >= 2)


BACK = [None] + [
    pairs(
        zh=lambda at, k=k: at["zh"] if near(at["zl"], k) else 1 - at["zh"],
        zl=lambda at, k=k: at["zl"] + k,
    )
    for k in range(1, ZL)
]


def send(x, table):
    return lax.ppermute(x, AXES, table)


def exchange(x, groups, axes="tp"):
    return lax.all_to_all(x, axes, 0, 0, tiled=True, axis_index_groups=groups)


def swap(x, me, tables):
    count = len(tables)
    out = [lax.dynamic_index_in_dim(x, (me + k) % count, 0, keepdims=False) for k in range(count)]
    got = jnp.stack([out[0]] + [send(out[k], tables[k]) for k in range(1, count)])
    return jnp.stack(
        [lax.dynamic_index_in_dim(got, (me - k) % count, 0, keepdims=False) for k in range(count)]
    )


def turn(cache_rows, position_ids, first_col):
    column = first_col + jnp.arange(cache_rows.shape[1], dtype=jnp.int32)
    within = column % (2 * HD)
    is_key = within < HD
    exponent = jnp.where(is_key, within - within % 2, 0).astype(F32) / HD
    frequency = jnp.power(F32(THETA), -exponent)
    angles = position_ids[:, None] * frequency[None, :]
    even = (column % 2 == 0)[None, :]
    other = jnp.where(even, -jnp.roll(cache_rows, -1, axis=1), jnp.roll(cache_rows, 1, axis=1))
    turned = cache_rows * jnp.cos(angles) + other * jnp.sin(angles)
    return jnp.where(is_key[None, :], turned, cache_rows)


def shards(
    residual, queries, keys_values, out_weight, norm_gain, cache_weight, positions, keep_rows, kept_count
):
    rows = residual.shape[0]
    ctx = lax.axis_index("ctx")
    tp = lax.axis_index("tp")
    zl, core = ctx // CORES, ctx % CORES
    zh, plane = tp // (NX * NY), tp % (NX * NY)
    x, y = plane // NY, plane % NY
    first = core == 0

    local = jnp.arange(rows, dtype=jnp.int32)
    order = jnp.where(local < kept_count[0], local, -1)
    hits = keep_rows[:, None] == local[None, :]
    rank = jnp.sum(jnp.where(hits, order[:, None], 0), axis=0)
    meta = jnp.stack([rank, positions // 128, positions % 128], axis=1).astype(BF)
    meta = jnp.pad(meta, ((0, 0), (0, 125)))
    mine = jnp.concatenate([queries, residual, meta], axis=1)

    head = zh * (KVH // ZH) + plane // NY
    far_head = (1 - zh) * (KVH // ZH) + plane // NY
    own_kv = lax.dynamic_slice_in_dim(keys_values, head * 2 * HD, 2 * HD, 1)
    far_kv = lax.dynamic_slice_in_dim(keys_values, far_head * 2 * HD, 2 * HD, 1)
    sent = {4: jnp.where(zl >= 2, own_kv, far_kv)}
    blocks = [own_kv] + [send(sent.get(k, own_kv if k < 4 else far_kv), BACK[k]) for k in range(1, ZL)]

    kept_rows = lax.dynamic_slice_in_dim(out_weight, core * HD, HD, 0)
    given_rows = lax.dynamic_slice_in_dim(out_weight, (1 - core) * HD, HD, 0)
    taken_rows = send(given_rows, CORE)
    weight = jnp.concatenate(
        [jnp.where(first, kept_rows, taken_rows), jnp.where(first, taken_rows, kept_rows)], axis=1
    )
    weight = weight.reshape(HD, NY, 256).transpose(1, 0, 2)
    weight = jnp.broadcast_to(weight[None], (4,) + weight.shape).reshape(4 * NY, HD, 256)
    weight, mine = lax.optimization_barrier((weight, mine))
    quad = exchange(weight, QUADS, AXES).reshape(NX, NY * HD, 256)
    theirs = send(mine, CORE)

    pair = jnp.where(first, jnp.concatenate([mine, theirs]), jnp.concatenate([theirs, mine]))
    pair_rank = pair[:, 512].astype(jnp.int32)
    count0 = jnp.sum((pair_rank[:rows] >= 0).astype(jnp.int32))
    pair_row = jnp.arange(2 * rows, dtype=jnp.int32)
    pair_rank = jnp.where(pair_rank >= 0, pair_rank + jnp.where(pair_row >= rows, count0, 0), -1)
    wanted = core * OWN + jnp.arange(OWN, dtype=jnp.int32)
    chosen = wanted[:, None] == pair_rank[None, :]
    picked = jnp.dot(chosen.astype(BF), pair, preferred_element_type=F32)
    token = zl * 2 * rows + jnp.sum(jnp.where(chosen, pair_row[None, :], 0), axis=1)
    position = picked[:, 513] * 128.0 + picked[:, 514]
    query = picked[:, :256].astype(BF).reshape(OWN, 2, HD).transpose(1, 0, 2).reshape(2 * OWN, HD)
    own_residual = picked[:, 256:512].astype(BF)

    kv_mine = jnp.concatenate(lax.optimization_barrier(blocks))
    kv_theirs = send(kv_mine, CORE)
    key_row = jnp.arange(ZL * rows, dtype=jnp.int32)
    key_token = (zl - key_row // rows) * 2 * rows + key_row % rows
    query_token = jnp.concatenate([token, token])

    def scored(kv, offset):
        scores = lax.dot_general(query, kv[:, :HD], (((1,), (1,)), ((), ())), preferred_element_type=F32)
        at = key_token + offset
        visible = (at[None, :] <= query_token[:, None]) & (at >= 0)[None, :]
        return jnp.where(visible, scores * (1.0 / math.sqrt(HD)), -1e30)

    score_a = scored(kv_mine, core * rows)
    score_b = scored(kv_theirs, (1 - core) * rows)
    top = jnp.maximum(jnp.max(score_a, axis=1), jnp.max(score_b, axis=1))[:, None]
    prob_a, prob_b = jnp.exp(score_a - top), jnp.exp(score_b - top)
    total = jnp.sum(prob_a, axis=1) + jnp.sum(prob_b, axis=1)
    mixed = jnp.dot(prob_a.astype(BF), kv_mine[:, HD:], preferred_element_type=F32) + jnp.dot(
        prob_b.astype(BF), kv_theirs[:, HD:], preferred_element_type=F32
    )
    attended = (mixed / total[:, None]).astype(BF)

    attended = attended.reshape(2, OWN, HD)
    attended = jnp.where(first, attended, attended[::-1])
    paired_residual = own_residual.reshape(OWN, 2, HD).transpose(1, 0, 2)
    partner = send(jnp.concatenate([attended, paired_residual]), FOUR)
    partner_residual = jnp.concatenate([partner[2], partner[3]], axis=1)
    partner = partner[:2]
    low = zl < 4
    both = jnp.concatenate([jnp.where(low, attended, partner), jnp.where(low, partner, attended)], axis=1)
    both, cache_weight, quad = lax.optimization_barrier((both, cache_weight, quad))
    quad_other = send(quad, CORE)
    cache_weight, quad_other = lax.optimization_barrier((cache_weight, quad_other))

    columns = cache_weight.shape[1]
    part = D // ZH
    gained = lax.dynamic_slice_in_dim(cache_weight, core * part, part, 0).astype(F32)
    gained = (gained * lax.dynamic_slice_in_dim(norm_gain, core * part, part, 0)[:, None]).astype(BF)
    gained = gained.T.reshape(columns, NX, NY, 256).transpose(1, 2, 0, 3)
    gained = swap(gained, x, NEXT_X).transpose(1, 0, 2, 3)

    heads = exchange(jnp.broadcast_to(both[None], (NY,) + both.shape), ALONG_Y)
    gained = swap(gained, y, NEXT_Y).transpose(1, 0, 2, 3).reshape(NX * NY, columns, 256)
    gained_other = send(gained, CORE)
    terms = 0.0
    for k, block in enumerate((quad, quad_other)):
        side = jnp.concatenate([heads[j, k] for j in range(NY)], axis=1)
        terms = terms + jnp.einsum("rk,ekn->ern", side, block, preferred_element_type=F32)
    terms = terms.astype(BF)
    summed = jnp.sum(exchange(terms, ALONG_X).reshape(NX, 2 * OWN, 256).astype(F32), axis=0)
    rest = jnp.concatenate(
        [jnp.where(low, own_residual, partner_residual), jnp.where(low, partner_residual, own_residual)]
    )
    holds = (zh == 0) == low
    summed = jnp.where(holds, summed + rest.astype(F32), summed).astype(BF).reshape(2, OWN, 256)
    halves = exchange(jnp.concatenate([summed, summed]), SETS, AXES).astype(F32)
    hidden0 = (halves[0] + halves[2]).astype(BF)
    hidden1 = (halves[1] + halves[3]).astype(BF)

    wide0, wide1 = hidden0.astype(F32), hidden1.astype(F32)
    square = jnp.sum(wide0 * wide0 + wide1 * wide1, axis=1, keepdims=True)
    square_high = square.astype(BF)
    square_low = (square - square_high.astype(F32)).astype(BF)
    parts = jnp.einsum(
        "rf,ecf->erc", jnp.where(first, hidden0, hidden1), gained, preferred_element_type=F32
    ) + jnp.einsum(
        "rf,ecf->erc", jnp.where(first, hidden1, hidden0), gained_other, preferred_element_type=F32
    )
    parts = parts.astype(BF)
    tail = jnp.pad(jnp.concatenate([square_high, square_low], axis=1), ((0, 0), (0, 128 - columns - 2)))
    message = jnp.concatenate([parts, jnp.broadcast_to(tail[None], (NX * NY,) + tail.shape)], axis=2)
    gathered = jnp.sum(exchange(message, PLANES).astype(F32), axis=0)
    square_total = gathered[:, columns] + gathered[:, columns + 1]
    cache_rows = gathered[:, :columns] * lax.rsqrt(square_total / D + EPS)[:, None]
    cache_rot = turn(cache_rows, position, tp * columns).astype(BF)

    own_rank = jnp.where(rank >= 0, rank + jnp.where(first, 0, count0), -1)
    put = (own_rank[:, None] == jnp.arange(PAIR_KEEP, dtype=jnp.int32)[None, :]).astype(BF)

    def back(mine):
        theirs = send(mine, CORE)
        kept = jnp.where(first, jnp.concatenate([mine, theirs]), jnp.concatenate([theirs, mine]))
        return jnp.dot(put, kept, preferred_element_type=F32).astype(BF)

    return back(jnp.where(zh == 0, hidden0, hidden1)), back(cache_rot)


def solution(mesh):
    in_specs = (
        P("ctx", "tp"),
        P("ctx", "tp"),
        P("ctx", None),
        P("tp", "ctx"),
        P(),
        P(None, "tp"),
        P("ctx"),
        P("ctx"),
        P("ctx"),
    )
    out_specs = (P("ctx", "tp"), P("ctx", "tp"))
    return jax.shard_map(shards, mesh=mesh, in_specs=in_specs, out_specs=out_specs, check_vma=False)
```

```python
import itertools
import math

import jax
import jax.numpy as jnp
from jax import lax
from jax.sharding import PartitionSpec as P

D = 8192
HQ = 64
KVH = 8
HD = 128
THETA = 1000000.0
EPS = 1e-06

ZL, CORES, ZH, NX, NY = 8, 2, 2, 4, 4
PAIR_KEEP = 320
OWN = PAIR_KEEP // 2
AXES = ("ctx", "tp")
BF = jnp.bfloat16
F32 = jnp.float32


def pairs(**moves):
    names = ("zh", "zl", "core", "x", "y")
    found = []
    for source in itertools.product(range(ZH), range(ZL), range(CORES), range(NX), range(NY)):
        at = dict(zip(names, source))
        target = {**at, **{name: move(at) for name, move in moves.items()}}
        if target["zl"] < ZL:
            found.append((place(*source), place(**target)))
    return found


def place(zh, zl, core, x, y):
    return (zl * CORES + core) * (ZH * NX * NY) + (zh * NX + x) * NY + y


CORE = pairs(core=lambda at: 1 - at["core"])
FOUR = pairs(zl=lambda at: at["zl"] ^ 4)
NEXT_X = [None] + [pairs(x=lambda at, k=k: (at["x"] + k) % NX) for k in (1, 2, 3)]
NEXT_Y = [None] + [pairs(y=lambda at, k=k: (at["y"] + k) % NY) for k in (1, 2, 3)]
PLANES = [[half * NX * NY + i for i in range(NX * NY)] for half in range(ZH)]
ALONG_Y = [[start * NY + y for y in range(NY)] for start in range(ZH * NX)]
ALONG_X = [[half * NX * NY + x * NY + y for x in range(NX)] for half in range(ZH) for y in range(NY)]
QUADS = [
    [place(zh, quad * 4 + low, core, x, y) for low in range(4) for y in range(NY)]
    for zh in range(ZH)
    for quad in range(2)
    for core in range(CORES)
    for x in range(NX)
]
SETS = [
    [place(zh, zl, core, x, y) for zh in range(ZH) for zl in (low, low + 4)]
    for low in range(4)
    for core in range(CORES)
    for x in range(NX)
    for y in range(NY)
]


def near(zl, k):
    return k < 4 or (k == 4 and zl >= 2)


BACK = [None] + [
    pairs(
        zh=lambda at, k=k: at["zh"] if near(at["zl"], k) else 1 - at["zh"],
        zl=lambda at, k=k: at["zl"] + k,
    )
    for k in range(1, ZL)
]


def send(x, table):
    return lax.ppermute(x, AXES, table)


def exchange(x, groups, axes="tp"):
    return lax.all_to_all(x, axes, 0, 0, tiled=True, axis_index_groups=groups)


def swap(x, me, tables):
    count = len(tables)
    out = [lax.dynamic_index_in_dim(x, (me + k) % count, 0, keepdims=False) for k in range(count)]
    got = jnp.stack([out[0]] + [send(out[k], tables[k]) for k in range(1, count)])
    return jnp.stack(
        [lax.dynamic_index_in_dim(got, (me - k) % count, 0, keepdims=False) for k in range(count)]
    )


def turn(cache_rows, position_ids, first_col):
    column = first_col + jnp.arange(cache_rows.shape[1], dtype=jnp.int32)
    within = column % (2 * HD)
    is_key = within < HD
    exponent = jnp.where(is_key, within - within % 2, 0).astype(F32) / HD
    frequency = jnp.power(F32(THETA), -exponent)
    angles = position_ids[:, None] * frequency[None, :]
    even = (column % 2 == 0)[None, :]
    other = jnp.where(even, -jnp.roll(cache_rows, -1, axis=1), jnp.roll(cache_rows, 1, axis=1))
    turned = cache_rows * jnp.cos(angles) + other * jnp.sin(angles)
    return jnp.where(is_key[None, :], turned, cache_rows)


def shards(
    residual, queries, keys_values, out_weight, norm_gain, cache_weight, positions, keep_rows, kept_count
):
    rows = residual.shape[0]
    ctx = lax.axis_index("ctx")
    tp = lax.axis_index("tp")
    zl, core = ctx // CORES, ctx % CORES
    zh, plane = tp // (NX * NY), tp % (NX * NY)
    x, y = plane // NY, plane % NY
    first = core == 0

    local = jnp.arange(rows, dtype=jnp.int32)
    order = jnp.where(local < kept_count[0], local, -1)
    hits = keep_rows[:, None] == local[None, :]
    rank = jnp.sum(jnp.where(hits, order[:, None], 0), axis=0)
    meta = jnp.stack([rank, positions // 128, positions % 128], axis=1).astype(BF)
    meta = jnp.pad(meta, ((0, 0), (0, 125)))
    mine = jnp.concatenate([queries, residual, meta], axis=1)

    head = zh * (KVH // ZH) + plane // NY
    far_head = (1 - zh) * (KVH // ZH) + plane // NY
    own_kv = lax.dynamic_slice_in_dim(keys_values, head * 2 * HD, 2 * HD, 1)
    far_kv = lax.dynamic_slice_in_dim(keys_values, far_head * 2 * HD, 2 * HD, 1)
    blocks = [own_kv] + [send(own_kv, BACK[k]) for k in (1, 2, 3)]
    mixed_kv = jnp.where(zl >= 2, own_kv, far_kv)
    far_kv, mixed_kv, _ = lax.optimization_barrier((far_kv, mixed_kv, blocks[1]))
    blocks += [send(mixed_kv, BACK[4])] + [send(far_kv, BACK[k]) for k in range(5, ZL)]

    kept_rows = lax.dynamic_slice_in_dim(out_weight, core * HD, HD, 0)
    given_rows = lax.dynamic_slice_in_dim(out_weight, (1 - core) * HD, HD, 0)
    taken_rows = send(given_rows, CORE)
    weight = jnp.concatenate(
        [jnp.where(first, kept_rows, taken_rows), jnp.where(first, taken_rows, kept_rows)], axis=1
    )
    weight = weight.reshape(HD, NY, 256).transpose(1, 0, 2)
    weight = jnp.broadcast_to(weight[None], (4,) + weight.shape).reshape(4 * NY, HD, 256)
    weight, mine = lax.optimization_barrier((weight, mine))
    quad = exchange(weight, QUADS, AXES).reshape(NX, NY * HD, 256)
    theirs = send(mine, CORE)

    pair = jnp.where(first, jnp.concatenate([mine, theirs]), jnp.concatenate([theirs, mine]))
    pair_rank = pair[:, 512].astype(jnp.int32)
    count0 = jnp.sum((pair_rank[:rows] >= 0).astype(jnp.int32))
    pair_row = jnp.arange(2 * rows, dtype=jnp.int32)
    pair_rank = jnp.where(pair_rank >= 0, pair_rank + jnp.where(pair_row >= rows, count0, 0), -1)
    wanted = core * OWN + jnp.arange(OWN, dtype=jnp.int32)
    chosen = wanted[:, None] == pair_rank[None, :]
    picked = jnp.dot(chosen.astype(BF), pair, preferred_element_type=F32)
    token = zl * 2 * rows + jnp.sum(jnp.where(chosen, pair_row[None, :], 0), axis=1)
    position = picked[:, 513] * 128.0 + picked[:, 514]
    query = picked[:, :256].astype(BF).reshape(OWN, 2, HD).transpose(1, 0, 2).reshape(2 * OWN, HD)
    own_residual = picked[:, 256:512].astype(BF)

    kv_mine = jnp.concatenate(lax.optimization_barrier(blocks))
    kv_theirs = send(kv_mine, CORE)
    key_row = jnp.arange(ZL * rows, dtype=jnp.int32)
    key_token = (zl - key_row // rows) * 2 * rows + key_row % rows
    query_token = jnp.concatenate([token, token])

    def scored(kv, offset):
        scores = lax.dot_general(query, kv[:, :HD], (((1,), (1,)), ((), ())), preferred_element_type=F32)
        at = key_token + offset
        visible = (at[None, :] <= query_token[:, None]) & (at >= 0)[None, :]
        return jnp.where(visible, scores * (1.0 / math.sqrt(HD)), -1e30)

    score_a = scored(kv_mine, core * rows)
    score_b = scored(kv_theirs, (1 - core) * rows)
    top = jnp.maximum(jnp.max(score_a, axis=1), jnp.max(score_b, axis=1))[:, None]
    prob_a, prob_b = jnp.exp(score_a - top), jnp.exp(score_b - top)
    total = jnp.sum(prob_a, axis=1) + jnp.sum(prob_b, axis=1)
    mixed = jnp.dot(prob_a.astype(BF), kv_mine[:, HD:], preferred_element_type=F32) + jnp.dot(
        prob_b.astype(BF), kv_theirs[:, HD:], preferred_element_type=F32
    )
    attended = (mixed / total[:, None]).astype(BF)

    attended = attended.reshape(2, OWN, HD)
    attended = jnp.where(first, attended, attended[::-1])
    paired_residual = own_residual.reshape(OWN, 2, HD).transpose(1, 0, 2)
    partner = send(jnp.concatenate([attended, paired_residual]), FOUR)
    partner_residual = jnp.concatenate([partner[2], partner[3]], axis=1)
    partner = partner[:2]
    low = zl < 4
    both = jnp.concatenate([jnp.where(low, attended, partner), jnp.where(low, partner, attended)], axis=1)
    both, cache_weight, quad = lax.optimization_barrier((both, cache_weight, quad))
    quad_other = send(quad, CORE)
    cache_weight, quad_other = lax.optimization_barrier((cache_weight, quad_other))

    columns = cache_weight.shape[1]
    part = D // ZH
    gained = lax.dynamic_slice_in_dim(cache_weight, core * part, part, 0).astype(F32)
    gained = (gained * lax.dynamic_slice_in_dim(norm_gain, core * part, part, 0)[:, None]).astype(BF)
    gained = gained.T.reshape(columns, NX, NY, 256).transpose(1, 2, 0, 3)
    gained = swap(gained, x, NEXT_X).transpose(1, 0, 2, 3)

    heads = exchange(jnp.broadcast_to(both[None], (NY,) + both.shape), ALONG_Y)
    gained = swap(gained, y, NEXT_Y).transpose(1, 0, 2, 3).reshape(NX * NY, columns, 256)
    gained_other = send(gained, CORE)
    terms = 0.0
    for k, block in enumerate((quad, quad_other)):
        side = jnp.concatenate([heads[j, k] for j in range(NY)], axis=1)
        terms = terms + jnp.einsum("rk,ekn->ern", side, block, preferred_element_type=F32)
    terms = terms.astype(BF)
    summed = jnp.sum(exchange(terms, ALONG_X).reshape(NX, 2 * OWN, 256).astype(F32), axis=0)
    rest = jnp.concatenate(
        [jnp.where(low, own_residual, partner_residual), jnp.where(low, partner_residual, own_residual)]
    )
    holds = (zh == 0) == low
    summed = jnp.where(holds, summed + rest.astype(F32), summed).astype(BF).reshape(2, OWN, 256)
    halves = exchange(jnp.concatenate([summed, summed]), SETS, AXES).astype(F32)
    hidden0 = (halves[0] + halves[2]).astype(BF)
    hidden1 = (halves[1] + halves[3]).astype(BF)

    wide0, wide1 = hidden0.astype(F32), hidden1.astype(F32)
    square = jnp.sum(wide0 * wide0 + wide1 * wide1, axis=1, keepdims=True)
    square_high = square.astype(BF)
    square_low = (square - square_high.astype(F32)).astype(BF)
    parts = jnp.einsum(
        "rf,ecf->erc", jnp.where(first, hidden0, hidden1), gained, preferred_element_type=F32
    ) + jnp.einsum(
        "rf,ecf->erc", jnp.where(first, hidden1, hidden0), gained_other, preferred_element_type=F32
    )
    parts = parts.astype(BF)
    tail = jnp.pad(jnp.concatenate([square_high, square_low], axis=1), ((0, 0), (0, 128 - columns - 2)))
    message = jnp.concatenate([parts, jnp.broadcast_to(tail[None], (NX * NY,) + tail.shape)], axis=2)
    gathered = jnp.sum(exchange(message, PLANES).astype(F32), axis=0)
    square_total = gathered[:, columns] + gathered[:, columns + 1]
    cache_rows = gathered[:, :columns] * lax.rsqrt(square_total / D + EPS)[:, None]
    cache_rot = turn(cache_rows, position, tp * columns).astype(BF)

    own_rank = jnp.where(rank >= 0, rank + jnp.where(first, 0, count0), -1)
    put = (own_rank[:, None] == jnp.arange(PAIR_KEEP, dtype=jnp.int32)[None, :]).astype(BF)

    def back(mine):
        theirs = send(mine, CORE)
        kept = jnp.where(first, jnp.concatenate([mine, theirs]), jnp.concatenate([theirs, mine]))
        return jnp.dot(put, kept, preferred_element_type=F32).astype(BF)

    return back(jnp.where(zh == 0, hidden0, hidden1)), back(cache_rot)


def solution(mesh):
    in_specs = (
        P("ctx", "tp"),
        P("ctx", "tp"),
        P("ctx", None),
        P("tp", "ctx"),
        P(),
        P(None, "tp"),
        P("ctx"),
        P("ctx"),
        P("ctx"),
    )
    out_specs = (P("ctx", "tp"), P("ctx", "tp"))
    return jax.shard_map(shards, mesh=mesh, in_specs=in_specs, out_specs=out_specs, check_vma=False)
```
